32 devices in a mesh: freq: 8 (over z, core), tile: 4 (over y, x).
Axes of the slice: x: 2, y: 2, z: 4, core: 2. Of those that a mesh axis runs over, the one named last changes fastest.
Arguments:
- recorded_seismograms: bfloat16 [2048, 16, 2048], P('freq', None, 'tile'), may hold values from -6 to 6
- left_bases: bfloat16 [8, 64, 8, 2, 32, 256], P('freq', None, 'tile'), may hold values from -1 to 1
- right_bases: bfloat16 [8, 64, 8, 2, 32, 256], P('freq', None, 'tile'), may hold values from -0.125 to 0.125
- rank_classes: int32 [8, 64, 8], P('freq', None, 'tile'), may hold values from 0 to 3
- owner: int32 [64], replicated, may hold values from 0 to 63, each once
Outputs:
- echo: float32 [8, 64, 2, 16, 256], P('freq', 'tile')
- adjoint_traces: bfloat16 [2048, 16, 2048], P('freq', None, 'tile')
The draws below stay inside these ranges and needn't reach their ends.
Inputs may be any that keep to these rules, and one draw needn't show every extreme that they name: `rank_classes`: rank class of a tile, 0 to 3. `owner`: each row tile stands at exactly one position.
All inputs are finite; a program needn't handle non-finite values.
Results may differ from the reference program's by a relative error of at most 0.03.
Values may be sent and summed in bfloat16 or wider, within the bound.
A program may use at most 128 MiB of HBM per device.

```python
import math
import jax
import jax.numpy as jnp
from jax import lax

TILE = 256
RMAX = 32
S = 16
RECORD_LENGTH = 2048
LOW_BIN = 8
RT = 64
FREQS = 8
CT = 8
NC = 2048


def set_ends(array, key, least, largest):
    place = [jax.random.randint(jax.random.fold_in(key, axis), (), 0, length) for axis, length in enumerate(array.shape)]
    main_axis = array.shape.index(max(array.shape))
    neighbour = place[:main_axis] + [(place[main_axis] + 1) % array.shape[main_axis]] + place[main_axis + 1:]
    return array.at[tuple(place)].set(least).at[tuple(neighbour)].set(largest)


def levels(stream_key, extent, pieces, smallest, largest):
    factor_of = 1.0
    for position, blocks in pieces:
        heights = jax.random.uniform(jax.random.fold_in(jax.random.fold_in(stream_key, 6), position), (blocks,), jnp.float32, smallest / len(pieces), largest / len(pieces))
        factor_of = factor_of * jnp.repeat(jnp.exp(heights), extent[position] // blocks).reshape((-1,) + (1,) * (len(extent) - 1 - position))
    return factor_of


def scatter_about(key, dims, scale, most, pieces=(), kind=jnp.bfloat16):
    drawn = jax.random.normal(key, dims, jnp.float32) * scale
    if len(pieces) > 0:
        drawn = levels(key, dims, pieces, -0.22, 0.18) * drawn
    return jnp.clip(drawn, min=-most, max=most).astype(kind)


def setup_inputs(seed: int = 0) -> dict:
    key_list = jax.random.split(jax.random.key(seed), 6)
    return {
        "recorded_seismograms": scatter_about(key_list[0], (RECORD_LENGTH, S, NC), 1.0, 6.0, ((0, 8), (2, 4))),
        "left_bases": scatter_about(key_list[1], (FREQS, RT, CT, 2, RMAX, TILE), RMAX ** -0.5, 1.0, ((0, 8), (2, 4))),
        "right_bases": scatter_about(key_list[2], (FREQS, RT, CT, 2, RMAX, TILE), (TILE * CT) ** -0.5, 0.125, ((0, 8), (2, 4))),
        "rank_classes": set_ends(jax.random.randint(key_list[3], (FREQS, RT, CT), 0, 4), jax.random.fold_in(key_list[3], 1), 0, 3).astype(jnp.int32),
        "owner": jax.random.permutation(key_list[4], RT).astype(jnp.int32),
    }


def fourier_kernel_matrices(spectral_bins, recording_moments):
    dyadic_matrix = (spectral_bins[:, None] * recording_moments[None, :]) % RECORD_LENGTH
    angles = dyadic_matrix.astype(jnp.float32) * (2.0 * math.pi / RECORD_LENGTH)
    return jnp.cos(angles), jnp.sin(angles)


def contract(form, first, second):
    return jnp.einsum(form, first.astype(jnp.float32), second.astype(jnp.float32))


def rounded(values):
    return lax.optimization_barrier(values.astype(jnp.bfloat16)).astype(jnp.float32)


def one_frequency(inputs):
    spectrum, left, right, kept, order = inputs
    left_real, left_imag = left[:, :, 0], left[:, :, 1]
    right_real, right_imag = right[:, :, 0], right[:, :, 1]
    spec_real, spec_imag = spectrum[0], spectrum[1]
    fwd_real = contract("ijrt,sjt->ijrs", right_real, spec_real) - contract("ijrt,sjt->ijrs", right_imag, spec_imag)
    fwd_imag = contract("ijrt,sjt->ijrs", right_real, spec_imag) + contract("ijrt,sjt->ijrs", right_imag, spec_real)
    fwd_real = rounded(fwd_real * kept)
    fwd_imag = rounded(fwd_imag * kept)
    out_real = contract("ijrt,ijrs->ist", left_real, fwd_real) - contract("ijrt,ijrs->ist", left_imag, fwd_imag)
    out_imag = contract("ijrt,ijrs->ist", left_real, fwd_imag) + contract("ijrt,ijrs->ist", left_imag, fwd_real)
    forward = jnp.stack([out_real, out_imag], 1)
    rows_real = rounded(out_real)
    rows_imag = rounded(out_imag)
    adj_real = contract("ijrt,ist->ijrs", left_real, rows_real) + contract("ijrt,ist->ijrs", left_imag, rows_imag)
    adj_imag = contract("ijrt,ist->ijrs", left_real, rows_imag) - contract("ijrt,ist->ijrs", left_imag, rows_real)
    adj_real = rounded(adj_real * kept)
    adj_imag = rounded(adj_imag * kept)
    col_real = contract("ijrt,ijrs->sjt", right_real, adj_real) + contract("ijrt,ijrs->sjt", right_imag, adj_imag)
    col_imag = contract("ijrt,ijrs->sjt", right_real, adj_imag) - contract("ijrt,ijrs->sjt", right_imag, adj_real)
    adjoint = jnp.stack([col_real, col_imag], 0).reshape(2, S, NC).astype(jnp.bfloat16)
    return jnp.take(forward, order, axis=0), adjoint


def reference(recorded_seismograms, left_bases, right_bases, rank_classes, owner):
    spectral_bins = LOW_BIN + jnp.arange(FREQS, dtype=jnp.int32)
    recording_moments = jnp.arange(RECORD_LENGTH, dtype=jnp.int32)
    cosinusoid_entries, sinusoid_matrix = fourier_kernel_matrices(spectral_bins, recording_moments)
    flat = recorded_seismograms.astype(jnp.float32).reshape(RECORD_LENGTH, S * NC)
    highest = lax.Precision.HIGHEST
    spec_real = jnp.dot(cosinusoid_entries, flat, precision=highest) * RECORD_LENGTH ** -0.5
    spec_imag = -jnp.dot(sinusoid_matrix, flat, precision=highest) * RECORD_LENGTH ** -0.5
    spectra = jnp.stack([spec_real, spec_imag], 1).reshape(FREQS, 2, S, CT, TILE).astype(jnp.bfloat16)
    limits = (rank_classes + 1) * (RMAX // 4)
    kept = (jnp.arange(RMAX, dtype=jnp.int32)[None, None, None, :] < limits[..., None]).astype(jnp.float32)[..., None]
    orders = jnp.broadcast_to(owner, (FREQS, RT))
    echo, adjoint = lax.map(one_frequency, (spectra, left_bases, right_bases, kept, orders))
    adjoint = adjoint.astype(jnp.float32)
    synth = jnp.einsum("ft,fsc->tsc", cosinusoid_entries, adjoint[:, 0], precision=highest)
    synth = synth - jnp.einsum("ft,fsc->tsc", sinusoid_matrix, adjoint[:, 1], precision=highest)
    return echo, (synth * FREQS ** -0.5).astype(jnp.bfloat16)
```

```python
import functools
import math

import jax
import jax.numpy as jnp
import numpy as np
from jax import lax
from jax.experimental import pallas as pl
from jax.experimental.pallas import tpu as pltpu
from jax.sharding import PartitionSpec as P

TILE = 256
RMAX = 32
S = 16
RECORD_LENGTH = 2048
LOW_BIN = 8
GROUP = 4
F32 = jnp.float32
BF16 = jnp.bfloat16
MESH = pl.DeviceIdType.MESH


def trig_tables(shards, count, freqs):
    bins = LOW_BIN + np.arange(freqs)
    angles = (bins[:, None] * np.arange(shards * count)[None, :] % RECORD_LENGTH) * (
        2.0 * math.pi / RECORD_LENGTH
    )
    both = np.stack([np.cos(angles), -np.sin(angles)], 1)
    both = both.reshape(2 * freqs, shards, count)
    ahead = np.repeat(both.transpose(1, 0, 2), S, axis=2)
    back = np.repeat(both.transpose(1, 2, 0), S, axis=2)
    return jnp.asarray(ahead, BF16), jnp.asarray(back, BF16)


def partner(me, off, size):
    out = me
    bit = 1
    while bit < size:
        if off & bit:
            out = out + (1 - 2 * ((me // bit) % 2)) * bit
        bit *= 2
    return out


def nt_dot(a, b):
    return lax.dot_general(a, b, (((1,), (1,)), ((), ())), preferred_element_type=F32)


def nn_dot(a, b):
    return jnp.dot(a, b, preferred_element_type=F32)


def apply_kernel(
    nf,
    nt,
    x_hbm,
    l_hbm,
    r_hbm,
    rank_ref,
    owner_ref,
    ahead_hbm,
    echo_ref,
    spec_out,
    x_ref,
    l_ref,
    r_ref,
    ahead_ref,
    a_ref,
    acc_ref,
    part_ref,
    rs_ref,
    s_ref,
    send_ref,
    recv_ref,
    own_ref,
    rows_ref,
    adj_ref,
    gath_ref,
    load_sem,
    rs_send,
    rs_recv,
    row_send,
    row_recv,
    ag_send,
    ag_recv,
    sp_send,
    sp_recv,
):
    me_f = lax.axis_index("freq")
    me_t = lax.axis_index("tile")
    count = x_ref.shape[0]
    cols = x_ref.shape[2]
    col_tiles = l_ref.shape[1]
    freqs = part_ref.shape[0]
    npos = own_ref.shape[0]
    quads = npos // GROUP
    chunks = 4
    step_t = count // chunks
    kk = step_t * S

    ahead_copy = pltpu.make_async_copy(ahead_hbm.at[me_f], ahead_ref, load_sem.at[0])
    ahead_copy.start()
    x_copies = []
    for n in range(chunks):
        cp = pltpu.make_async_copy(
            x_hbm.at[pl.ds(n * step_t, step_t)], x_ref.at[pl.ds(n * step_t, step_t)], load_sem.at[1 + n]
        )
        cp.start()
        x_copies.append(cp)
    r_copy = pltpu.make_async_copy(r_hbm, r_ref, load_sem.at[1 + chunks])
    r_copy.start()
    l_copy = pltpu.make_async_copy(l_hbm, l_ref, load_sem.at[2 + chunks])
    l_copy.start()

    barrier = pltpu.get_barrier_semaphore()
    for off in range(1, nf):
        pl.semaphore_signal(
            barrier, inc=1, device_id=(partner(me_f, off, nf), me_t), device_id_type=MESH
        )
    for off in range(1, nt):
        pl.semaphore_signal(
            barrier, inc=1, device_id=(me_f, partner(me_t, off, nt)), device_id_type=MESH
        )

    ahead_copy.wait()
    diag = lax.broadcasted_iota(jnp.int32, (S, kk), 1) % S == lax.broadcasted_iota(
        jnp.int32, (S, kk), 0
    )
    for n in range(chunks):
        table = ahead_ref[:, n * kk : (n + 1) * kk].astype(F32)
        for k in range(2 * freqs):
            row = jnp.broadcast_to(table[k : k + 1], (S, kk))
            a_ref[k * S : (k + 1) * S, n * kk : (n + 1) * kk] = jnp.where(diag, row, 0.0).astype(
                BF16
            )
    for n in range(chunks):
        x_copies[n].wait()
    total = nn_dot(a_ref[...], x_ref[...].reshape(count * S, cols)) * RECORD_LENGTH**-0.5
    total = total.reshape(freqs, 2 * S, cols)
    acc_ref[...] = total
    part_ref[...] = total.astype(BF16)

    pl.semaphore_wait(barrier, nf + nt - 2)
    rs_copies = []
    for off in range(nf - 1, 0, -1):
        to = partner(me_f, off, nf)
        cp = pltpu.make_async_remote_copy(
            src_ref=part_ref.at[to],
            dst_ref=rs_ref.at[off],
            send_sem=rs_send.at[off],
            recv_sem=rs_recv.at[off],
            device_id=(to, me_t),
            device_id_type=MESH,
        )
        cp.start()
        rs_copies.append((off, cp))
    adj_ref[...] = jnp.zeros_like(adj_ref)
    r_copy.wait()
    l_copy.wait()
    spectra = acc_ref[me_f]
    for off, cp in rs_copies:
        cp.wait()
        spectra = spectra + rs_ref[off].astype(F32)
    s_ref[...] = spectra.astype(BF16)

    width = GROUP * RMAX
    lane = lax.broadcasted_iota(jnp.int32, (1, width), 1)
    lane_m = lane // RMAX
    lane_r = lane % RMAX
    block = (
        lax.broadcasted_iota(jnp.int32, (GROUP * 2 * S, width), 0) // (2 * S)
        == lax.broadcasted_iota(jnp.int32, (GROUP * 2 * S, width), 1) // RMAX
    )

    def gather(ref, idx, j, c):
        return [ref[i, j, c] for i in idx]

    def kept(idx, j):
        limit = jnp.zeros((1, width), jnp.int32)
        for m, i in enumerate(idx):
            value = (rank_ref[i * col_tiles + j] + 1) * (RMAX // 4)
            limit = jnp.where(lane_m == m, value, limit)
        return jnp.where(lane_r < limit, 1.0, 0.0).astype(F32)

    def forward(base):
        idx = [owner_ref[base + m] for m in range(GROUP)]
        left, weights = [], []
        for j in range(col_tiles):
            right = jnp.concatenate(gather(r_ref, idx, j, 0) + gather(r_ref, idx, j, 1), 0)
            p = nt_dot(s_ref[:, j * TILE : (j + 1) * TILE], right)
            keep = kept(idx, j)
            wr = (p[:S, :width] - p[S:, width:]) * keep
            wi = (p[S:, :width] + p[:S, width:]) * keep
            for first in ([wr, wi], [-wi, wr]):
                tiled = jnp.concatenate(first * GROUP, 0)
                weights.append(jnp.where(block, tiled, 0.0).astype(BF16))
            left += gather(l_ref, idx, j, 0) + gather(l_ref, idx, j, 1)
        return nn_dot(jnp.concatenate(weights, 1), jnp.concatenate(left, 0))

    def backward(base, rows):
        idx = [owner_ref[base + m] for m in range(GROUP)]
        left = []
        for j in range(col_tiles):
            left += gather(l_ref, idx, j, 0) + gather(l_ref, idx, j, 1)
        p = nt_dot(rows, jnp.concatenate(left, 0))
        for j in range(col_tiles):
            sums = []
            for c in range(2):
                at = (2 * j + c) * width
                q = jnp.where(block, p[:, at : at + width], 0.0)
                g = q[: 2 * S]
                for m in range(1, GROUP):
                    g = g + q[2 * S * m : 2 * S * (m + 1)]
                sums.append(g)
            keep = kept(idx, j)
            ar = (sums[0][:S] + sums[1][S:]) * keep
            ai = (sums[0][S:] - sums[1][:S]) * keep
            lhs = jnp.concatenate(
                [jnp.concatenate([ar, ai], 0), jnp.concatenate([ai, -ar], 0)], 1
            ).astype(BF16)
            right = jnp.concatenate(gather(r_ref, idx, j, 0) + gather(r_ref, idx, j, 1), 0)
            adj_ref[:, j * TILE : (j + 1) * TILE] += nn_dot(lhs, right)

    def row_copy(off, q):
        return pltpu.make_async_remote_copy(
            src_ref=send_ref.at[off - 1, q],
            dst_ref=recv_ref.at[off - 1, q],
            send_sem=row_send.at[off - 1, q],
            recv_sem=row_recv.at[off - 1, q],
            device_id=(me_f, partner(me_t, off, nt)),
            device_id_type=MESH,
        )

    def rows_copy(off, q):
        return pltpu.make_async_remote_copy(
            src_ref=rows_ref.at[0, q],
            dst_ref=rows_ref.at[off, q],
            send_sem=ag_send.at[off - 1, q],
            recv_sem=ag_recv.at[off - 1, q],
            device_id=(me_f, partner(me_t, off, nt)),
            device_id_type=MESH,
        )

    @pl.loop(0, quads)
    def _(q):
        for off in range(nt - 1, 0, -1):
            out = forward(partner(me_t, off, nt) * npos + q * GROUP)
            send_ref[off - 1, q] = out.astype(BF16)
            row_copy(off, q).start()
        out = forward(me_t * npos + q * GROUP)
        own_ref[pl.ds(q * GROUP, GROUP)] = out.reshape(GROUP, 2 * S, TILE)

    @pl.loop(0, quads)
    def _(q):
        rows = own_ref[pl.ds(q * GROUP, GROUP)].reshape(GROUP * 2 * S, TILE)
        for off in range(1, nt):
            row_copy(off, q).wait()
            rows = rows + recv_ref[off - 1, q].astype(F32)
        echo_ref[pl.ds(q * GROUP, GROUP)] = rows.reshape(GROUP, 2 * S, TILE)
        low = rows.astype(BF16)
        rows_ref[0, q] = low
        for off in range(nt - 1, 0, -1):
            rows_copy(off, q).start()
        backward(me_t * npos + q * GROUP, low)

    @pl.loop(0, quads)
    def _(q):
        for off in range(1, nt):
            rows_copy(off, q).wait()
            backward(partner(me_t, off, nt) * npos + q * GROUP, rows_ref[off, q])

    gath_ref[me_f] = adj_ref[...].astype(BF16)
    sp_copies = []
    for off in range(nf - 1, 0, -1):
        cp = pltpu.make_async_remote_copy(
            src_ref=gath_ref.at[me_f],
            dst_ref=gath_ref.at[me_f],
            send_sem=sp_send.at[off],
            recv_sem=sp_recv.at[off],
            device_id=(partner(me_f, off, nf), me_t),
            device_id_type=MESH,
        )
        cp.start()
        sp_copies.append(cp)
    for cp in sp_copies:
        cp.wait()
    spec_out[...] = gath_ref[...]


def synthesis_kernel(freqs, spec_ref, echo_in, back_hbm, echo_out, out_hbm, back_ref, out_ref, sem):
    me_f = lax.axis_index("freq")
    count, cols = out_hbm.shape[0], out_hbm.shape[2]
    chunks = out_ref.shape[0]
    step_t = count // chunks
    lanes = back_ref.shape[1]
    back_copy = pltpu.make_async_copy(back_hbm.at[me_f], back_ref, sem.at[0])
    back_copy.start()
    echo_copy = pltpu.make_async_copy(echo_in, echo_out, sem.at[1])
    echo_copy.start()
    diag = lax.broadcasted_iota(jnp.int32, (S, lanes), 1) % S == lax.broadcasted_iota(
        jnp.int32, (S, lanes), 0
    )
    spec = spec_ref[...].reshape(lanes, cols)
    back_copy.wait()
    copies = []
    for n in range(chunks):
        table = back_ref[n * step_t : (n + 1) * step_t].astype(F32)
        spread = jnp.where(diag[None], table[:, None, :], 0.0).astype(BF16)
        out = nn_dot(spread.reshape(step_t * S, lanes), spec) * freqs**-0.5
        out_ref[n] = out.reshape(step_t, S, cols).astype(BF16)
        cp = pltpu.make_async_copy(
            out_ref.at[n], out_hbm.at[pl.ds(n * step_t, step_t)], sem.at[2 + n]
        )
        cp.start()
        copies.append(cp)
    for cp in copies:
        cp.wait()
    echo_copy.wait()


def shards(nf, nt, recorded_seismograms, left_bases, right_bases, rank_classes, owner):
    count, _, cols = recorded_seismograms.shape
    per_device, row_tiles, col_tiles = left_bases.shape[:3]
    assert per_device == 1
    freqs = per_device * nf
    npos = row_tiles // nt
    quads = npos // GROUP
    left = left_bases.reshape(left_bases.shape[1:])
    right = right_bases.reshape(right_bases.shape[1:])
    ahead, back = trig_tables(nf, count, freqs)
    vmem = pl.BlockSpec(memory_space=pltpu.VMEM)
    smem = pl.BlockSpec(memory_space=pltpu.SMEM)
    hbm = pl.BlockSpec(memory_space=pl.ANY)
    dma = pltpu.SemaphoreType.DMA
    block = (GROUP * 2 * S, TILE)
    echo, spec = pl.pallas_call(
        functools.partial(apply_kernel, nf, nt),
        out_shape=(
            jax.ShapeDtypeStruct((npos, 2 * S, TILE), F32),
            jax.ShapeDtypeStruct((freqs, 2 * S, cols), BF16),
        ),
        in_specs=[hbm, hbm, hbm, smem, smem, hbm],
        out_specs=(vmem, vmem),
        scratch_shapes=[
            pltpu.VMEM(recorded_seismograms.shape, BF16),
            pltpu.VMEM(left.shape, BF16),
            pltpu.VMEM(right.shape, BF16),
            pltpu.VMEM(ahead.shape[1:], BF16),
            pltpu.VMEM((freqs * 2 * S, count * S), BF16),
            pltpu.VMEM((freqs, 2 * S, cols), F32),
            pltpu.VMEM((freqs, 2 * S, cols), BF16),
            pltpu.VMEM((nf, 2 * S, cols), BF16),
            pltpu.VMEM((2 * S, cols), BF16),
            pltpu.VMEM((nt - 1, quads) + block, BF16),
            pltpu.VMEM((nt - 1, quads) + block, BF16),
            pltpu.VMEM((npos, 2 * S, TILE), F32),
            pltpu.VMEM((nt, quads) + block, BF16),
            pltpu.VMEM((2 * S, cols), F32),
            pltpu.VMEM((freqs, 2 * S, cols), BF16),
            dma((7,)),
            dma((nf,)),
            dma((nf,)),
            dma((nt - 1, quads)),
            dma((nt - 1, quads)),
            dma((nt - 1, quads)),
            dma((nt - 1, quads)),
            dma((nf,)),
            dma((nf,)),
        ],
        compiler_params=pltpu.CompilerParams(
            collective_id=0, has_side_effects=True, vmem_limit_bytes=40 * 2**20
        ),
        name="apply",
    )(recorded_seismograms, left, right, rank_classes.reshape(-1), owner, ahead)
    chunks = 4
    echo, synth = pl.pallas_call(
        functools.partial(synthesis_kernel, freqs),
        out_shape=(
            jax.ShapeDtypeStruct(echo.shape, F32),
            jax.ShapeDtypeStruct(recorded_seismograms.shape, BF16),
        ),
        in_specs=[vmem, hbm, hbm],
        out_specs=(hbm, hbm),
        scratch_shapes=[
            pltpu.VMEM(back.shape[1:], BF16),
            pltpu.VMEM((chunks, count // chunks, S, cols), BF16),
            dma((2 + chunks,)),
        ],
        compiler_params=pltpu.CompilerParams(vmem_limit_bytes=40 * 2**20),
        name="synthesis",
    )(spec, echo, back)
    return echo.reshape(1, npos, 2, S, TILE), synth


def solution(mesh):
    nf, nt = mesh.shape["freq"], mesh.shape["tile"]
    in_specs = (
        P("freq", None, "tile"),
        P("freq", None, "tile", None, None, None),
        P("freq", None, "tile", None, None, None),
        P("freq", None, "tile"),
        P(),
    )
    out_specs = (P("freq", "tile", None, None, None), P("freq", None, "tile"))
    return jax.shard_map(
        functools.partial(shards, nf, nt),
        mesh=mesh,
        in_specs=in_specs,
        out_specs=out_specs,
        check_vma=False,
    )
```

```python
import functools
import math

import jax
import jax.numpy as jnp
import numpy as np
from jax import lax
from jax.experimental import pallas as pl
from jax.experimental.pallas import tpu as pltpu
from jax.sharding import PartitionSpec as P

TILE = 256
RMAX = 32
S = 16
RECORD_LENGTH = 2048
LOW_BIN = 8
GROUP = 4
F32 = jnp.float32
BF16 = jnp.bfloat16
MESH = pl.DeviceIdType.MESH


def trig_tables(shards, count, freqs):
    bins = LOW_BIN + np.arange(freqs)
    angles = (bins[:, None] * np.arange(shards * count)[None, :] % RECORD_LENGTH) * (
        2.0 * math.pi / RECORD_LENGTH
    )
    both = np.stack([np.cos(angles), -np.sin(angles)], 1)
    both = both.reshape(2 * freqs, shards, count)
    near = both.reshape(freqs // 2, 2, 2, shards, count).swapaxes(0, 1)
    near = near.reshape(2 * freqs, shards, count)
    ahead = np.repeat(near.transpose(1, 0, 2), S, axis=2)
    back = np.repeat(both.transpose(1, 2, 0), S, axis=2)
    return jnp.asarray(ahead, BF16), jnp.asarray(back, BF16)


def partner(me, off, size):
    out = me
    bit = 1
    while bit < size:
        if off & bit:
            out = out + (1 - 2 * ((me // bit) % 2)) * bit
        bit *= 2
    return out


def nt_dot(a, b):
    return lax.dot_general(a, b, (((1,), (1,)), ((), ())), preferred_element_type=F32)


def nn_dot(a, b):
    return jnp.dot(a, b, preferred_element_type=F32)


def apply_kernel(
    nf,
    nt,
    x_hbm,
    l_hbm,
    r_hbm,
    rank_ref,
    owner_ref,
    ahead_hbm,
    echo_ref,
    spec_out,
    x_ref,
    l_ref,
    r_ref,
    ahead_ref,
    a_ref,
    acc_ref,
    part_ref,
    pair_ref,
    rs_ref,
    s_ref,
    send_ref,
    recv_ref,
    mid_ref,
    own_ref,
    rows_ref,
    adj_ref,
    gath_ref,
    load_sem,
    pair_sem,
    rs_send,
    rs_recv,
    row_send,
    row_recv,
    ag_send,
    ag_recv,
    sp_send,
    sp_recv,
):
    me_f = lax.axis_index("freq")
    me_t = lax.axis_index("tile")
    nz = nf // 2
    me_z, core = me_f // 2, me_f % 2
    sibling = me_f + 1 - 2 * core
    count = x_ref.shape[0]
    cols = x_ref.shape[2]
    col_tiles = l_ref.shape[1]
    freqs = nf
    npos = own_ref.shape[0]
    quads = npos // GROUP
    chunks = 4
    step_t = count // chunks
    kk = step_t * S

    ahead_copy = pltpu.make_async_copy(ahead_hbm.at[me_f], ahead_ref, load_sem.at[0])
    ahead_copy.start()
    x_copies = []
    for n in range(chunks):
        cp = pltpu.make_async_copy(
            x_hbm.at[pl.ds(n * step_t, step_t)], x_ref.at[pl.ds(n * step_t, step_t)], load_sem.at[1 + n]
        )
        cp.start()
        x_copies.append(cp)
    r_copy = pltpu.make_async_copy(r_hbm, r_ref, load_sem.at[1 + chunks])
    r_copy.start()
    l_copy = pltpu.make_async_copy(l_hbm, l_ref, load_sem.at[2 + chunks])
    l_copy.start()

    barrier = pltpu.get_barrier_semaphore()
    pl.semaphore_signal(barrier, inc=1, device_id=(sibling, me_t), device_id_type=MESH)
    for off in range(1, nz):
        pl.semaphore_signal(
            barrier,
            inc=1,
            device_id=(2 * partner(me_z, off, nz) + core, me_t),
            device_id_type=MESH,
        )
    two_level = nt == 4 and quads % 2 == 0
    offsets = (1, 2) if two_level else range(1, nt)
    barrier_count = nz + len(offsets)
    for off in offsets:
        pl.semaphore_signal(
            barrier, inc=1, device_id=(me_f, partner(me_t, off, nt)), device_id_type=MESH
        )

    ahead_copy.wait()
    diag = lax.broadcasted_iota(jnp.int32, (S, kk), 1) % S == lax.broadcasted_iota(
        jnp.int32, (S, kk), 0
    )
    total = 0.0
    for n in range(chunks):
        table = ahead_ref[:, n * kk : (n + 1) * kk].astype(F32)
        for k in range(2 * freqs):
            row = jnp.broadcast_to(table[k : k + 1], (S, kk))
            a_ref[k * S : (k + 1) * S, n * kk : (n + 1) * kk] = jnp.where(diag, row, 0.0).astype(
                BF16
            )
        x_copies[n].wait()
        block_x = x_ref[n * step_t : (n + 1) * step_t].reshape(kk, cols)
        total = total + nn_dot(a_ref[:, n * kk : (n + 1) * kk], block_x)
    total = (total * RECORD_LENGTH**-0.5).reshape(2, nz, 2 * S, cols)
    acc_ref[...] = total
    part_ref[...] = total.astype(BF16)

    pl.semaphore_wait(barrier, barrier_count)
    pair_copy = pltpu.make_async_remote_copy(
        src_ref=part_ref.at[1 - core],
        dst_ref=pair_ref,
        send_sem=pair_sem.at[0],
        recv_sem=pair_sem.at[1],
        device_id=(sibling, me_t),
        device_id_type=MESH,
    )
    pair_copy.start()
    adj_ref[...] = jnp.zeros_like(adj_ref)
    r_copy.wait()
    l_copy.wait()
    pair_copy.wait()
    summed = acc_ref[core] + pair_ref[...].astype(F32)
    acc_ref[core] = summed
    part_ref[core] = summed.astype(BF16)
    rs_copies = []
    for off in range(nz - 1, 0, -1):
        to = partner(me_z, off, nz)
        cp = pltpu.make_async_remote_copy(
            src_ref=part_ref.at[core, to],
            dst_ref=rs_ref.at[off],
            send_sem=rs_send.at[off],
            recv_sem=rs_recv.at[off],
            device_id=(2 * to + core, me_t),
            device_id_type=MESH,
        )
        cp.start()
        rs_copies.append((off, cp))
    spectra = acc_ref[core, me_z]
    for off, cp in reversed(rs_copies):
        cp.wait()
        spectra = spectra + rs_ref[off].astype(F32)
    s_ref[...] = spectra.astype(BF16)

    width = GROUP * RMAX
    lane = lax.broadcasted_iota(jnp.int32, (1, width), 1)
    lane_m = lane // RMAX
    lane_r = lane % RMAX
    block = (
        lax.broadcasted_iota(jnp.int32, (GROUP * 2 * S, width), 0) // (2 * S)
        == lax.broadcasted_iota(jnp.int32, (GROUP * 2 * S, width), 1) // RMAX
    )

    def gather(ref, idx, j, c):
        return [ref[i, j, c] for i in idx]

    def kept(idx, j):
        limit = jnp.zeros((1, width), jnp.int32)
        for m, i in enumerate(idx):
            value = (rank_ref[j, i] + 1) * (RMAX // 4)
            limit = jnp.where(lane_m == m, value, limit)
        return jnp.where(lane_r < limit, 1.0, 0.0).astype(F32)

    def forward(base):
        idx = [owner_ref[base + m] for m in range(GROUP)]
        left, weights = [], []
        for j in range(col_tiles):
            right = jnp.concatenate(gather(r_ref, idx, j, 0) + gather(r_ref, idx, j, 1), 0)
            p = nt_dot(s_ref[:, j * TILE : (j + 1) * TILE], right)
            keep = kept(idx, j)
            wr = (p[:S, :width] - p[S:, width:]) * keep
            wi = (p[S:, :width] + p[:S, width:]) * keep
            for first in ([wr, wi], [-wi, wr]):
                tiled = jnp.concatenate(first * GROUP, 0)
                weights.append(jnp.where(block, tiled, 0.0).astype(BF16))
            left += gather(l_ref, idx, j, 0) + gather(l_ref, idx, j, 1)
        return nn_dot(jnp.concatenate(weights, 1), jnp.concatenate(left, 0))

    def backward(base, rows):
        idx = [owner_ref[base + m] for m in range(GROUP)]
        left = []
        for j in range(col_tiles):
            left += gather(l_ref, idx, j, 0) + gather(l_ref, idx, j, 1)
        p = nt_dot(rows, jnp.concatenate(left, 0))
        for j in range(col_tiles):
            sums = []
            for c in range(2):
                at = (2 * j + c) * width
                q = jnp.where(block, p[:, at : at + width], 0.0)
                g = q[: 2 * S]
                for m in range(1, GROUP):
                    g = g + q[2 * S * m : 2 * S * (m + 1)]
                sums.append(g)
            keep = kept(idx, j)
            ar = (sums[0][:S] + sums[1][S:]) * keep
            ai = (sums[0][S:] - sums[1][:S]) * keep
            lhs = jnp.concatenate(
                [jnp.concatenate([ar, ai], 0), jnp.concatenate([ai, -ar], 0)], 1
            ).astype(BF16)
            right = jnp.concatenate(gather(r_ref, idx, j, 0) + gather(r_ref, idx, j, 1), 0)
            adj_ref[:, j * TILE : (j + 1) * TILE] += nn_dot(lhs, right)

    def row_copy(off, q):
        return pltpu.make_async_remote_copy(
            src_ref=send_ref.at[off - 1, q],
            dst_ref=recv_ref.at[off - 1, q],
            send_sem=row_send.at[off - 1, q],
            recv_sem=row_recv.at[off - 1, q],
            device_id=(me_f, partner(me_t, off, nt)),
            device_id_type=MESH,
        )

    def rows_copy(off, q):
        return pltpu.make_async_remote_copy(
            src_ref=rows_ref.at[0, q],
            dst_ref=rows_ref.at[off, q],
            send_sem=ag_send.at[off - 1, q],
            recv_sem=ag_recv.at[off - 1, q],
            device_id=(me_f, partner(me_t, off, nt)),
            device_id_type=MESH,
        )

    if two_level:

        def hop(src, dst, sems, k, q, off):
            return pltpu.make_async_remote_copy(
                src_ref=src,
                dst_ref=dst,
                send_sem=sems[0].at[k, q],
                recv_sem=sems[1].at[k, q],
                device_id=(me_f, partner(me_t, off, nt)),
                device_id_type=MESH,
            )

        def row_hop(k, q, off):
            return hop(send_ref.at[k, q], recv_ref.at[k, q], (row_send, row_recv), k, q, off)

        def ag_hop(k, q, src, off):
            return hop(rows_ref.at[src, q], rows_ref.at[k, q], (ag_send, ag_recv), k - 1, q, off)

        def base_of(off, q):
            return partner(me_t, off, nt) * npos + q * GROUP

        @pl.loop(0, quads // 2)
        def _(half):
            for k in range(2):
                for first in (1, 2):
                    q = 2 * half + first - 1
                    off = (3, first)[k]
                    send_ref[k, q] = forward(base_of(off, q)).astype(BF16)
                    row_hop(k, q, first).start()
            for first in (1, 2):
                q = 2 * half + first - 1
                mid_ref[q] = forward(base_of(3 - first, q))
                out = forward(base_of(0, q))
                own_ref[pl.ds(q * GROUP, GROUP)] = out.reshape(GROUP, 2 * S, TILE)

        @pl.loop(0, quads // 2)
        def _(half):
            for first in (1, 2):
                q = 2 * half + first - 1
                row_hop(0, q, first).wait()
                send_ref[2, q] = (mid_ref[q] + recv_ref[0, q].astype(F32)).astype(BF16)
                row_hop(2, q, 3 - first).start()

        @pl.loop(0, quads // 2)
        def _(half):
            for first in (1, 2):
                q = 2 * half + first - 1
                rows = own_ref[pl.ds(q * GROUP, GROUP)].reshape(GROUP * 2 * S, TILE)
                row_hop(1, q, first).wait()
                row_hop(2, q, 3 - first).wait()
                rows = rows + recv_ref[1, q].astype(F32) + recv_ref[2, q].astype(F32)
                echo_ref[pl.ds(q * GROUP, GROUP)] = rows.reshape(GROUP, 2 * S, TILE)
                low = rows.astype(BF16)
                rows_ref[0, q] = low
                ag_hop(first, q, 0, first).start()
                ag_hop(3 - first, q, 0, 3 - first).start()
                backward(base_of(0, q), low)

        @pl.loop(0, quads // 2)
        def _(half):
            for first in (1, 2):
                q = 2 * half + first - 1
                ag_hop(first, q, 0, first).wait()
                ag_hop(3, q, first, 3 - first).start()
                ag_hop(3 - first, q, 0, 3 - first).wait()
                backward(base_of(first, q), rows_ref[first, q])
                backward(base_of(3 - first, q), rows_ref[3 - first, q])

        @pl.loop(0, quads // 2)
        def _(half):
            for first in (1, 2):
                q = 2 * half + first - 1
                ag_hop(3, q, first, 3 - first).wait()
                backward(base_of(3, q), rows_ref[3, q])

    else:

        @pl.loop(0, quads)
        def _(q):
            for off in range(nt - 1, 0, -1):
                out = forward(partner(me_t, off, nt) * npos + q * GROUP)
                send_ref[off - 1, q] = out.astype(BF16)
                row_copy(off, q).start()
            out = forward(me_t * npos + q * GROUP)
            own_ref[pl.ds(q * GROUP, GROUP)] = out.reshape(GROUP, 2 * S, TILE)

        @pl.loop(0, quads)
        def _(q):
            rows = own_ref[pl.ds(q * GROUP, GROUP)].reshape(GROUP * 2 * S, TILE)
            for off in range(1, nt):
                row_copy(off, q).wait()
                rows = rows + recv_ref[off - 1, q].astype(F32)
            echo_ref[pl.ds(q * GROUP, GROUP)] = rows.reshape(GROUP, 2 * S, TILE)
            low = rows.astype(BF16)
            rows_ref[0, q] = low
            for off in range(nt - 1, 0, -1):
                rows_copy(off, q).start()
            backward(me_t * npos + q * GROUP, low)

        @pl.loop(0, quads)
        def _(q):
            for off in range(1, nt):
                rows_copy(off, q).wait()
                backward(partner(me_t, off, nt) * npos + q * GROUP, rows_ref[off, q])

    gath_ref[me_f] = adj_ref[...].astype(BF16)

    def spec_copy(n, at, to):
        return pltpu.make_async_remote_copy(
            src_ref=gath_ref.at[at],
            dst_ref=gath_ref.at[at],
            send_sem=sp_send.at[n],
            recv_sem=sp_recv.at[n],
            device_id=(to, me_t),
            device_id_type=MESH,
        )

    sp_copies = []
    for off in range(nz - 1, 0, -1):
        to = 2 * partner(me_z, off, nz) + core
        cp = spec_copy(off, me_f, to)
        cp.start()
        sp_copies.append((off, to, cp))
    last = [spec_copy(nz, me_f, sibling)]
    last[0].start()
    for off, to, cp in reversed(sp_copies):
        cp.wait()
        last.append(spec_copy(nz + off, to, sibling))
        last[-1].start()
    for cp in last:
        cp.wait()
    spec_out[...] = gath_ref[...]


def synthesis_kernel(freqs, spec_ref, echo_in, back_hbm, echo_out, out_hbm, back_ref, out_ref, sem):
    me_f = lax.axis_index("freq")
    count, cols = out_hbm.shape[0], out_hbm.shape[2]
    chunks = out_ref.shape[0]
    step_t = count // chunks
    lanes = back_ref.shape[1]
    back_copy = pltpu.make_async_copy(back_hbm.at[me_f], back_ref, sem.at[0])
    back_copy.start()
    echo_copy = pltpu.make_async_copy(echo_in, echo_out, sem.at[1])
    echo_copy.start()
    diag = lax.broadcasted_iota(jnp.int32, (S, lanes), 1) % S == lax.broadcasted_iota(
        jnp.int32, (S, lanes), 0
    )
    spec = spec_ref[...].reshape(lanes, cols)
    back_copy.wait()
    copies = []
    for n in range(chunks):
        table = back_ref[n * step_t : (n + 1) * step_t].astype(F32)
        spread = jnp.where(diag[None], table[:, None, :], 0.0).astype(BF16)
        out = nn_dot(spread.reshape(step_t * S, lanes), spec) * freqs**-0.5
        out_ref[n] = out.reshape(step_t, S, cols).astype(BF16)
        cp = pltpu.make_async_copy(
            out_ref.at[n], out_hbm.at[pl.ds(n * step_t, step_t)], sem.at[2 + n]
        )
        cp.start()
        copies.append(cp)
    for cp in copies:
        cp.wait()
    echo_copy.wait()


def shards(nf, nt, recorded_seismograms, left_bases, right_bases, rank_classes, owner):
    count, _, cols = recorded_seismograms.shape
    per_device, row_tiles, col_tiles = left_bases.shape[:3]
    assert per_device == 1
    freqs = per_device * nf
    npos = row_tiles // nt
    quads = npos // GROUP
    left = left_bases.reshape(left_bases.shape[1:])
    right = right_bases.reshape(right_bases.shape[1:])
    ahead, back = trig_tables(nf, count, freqs)
    vmem = pl.BlockSpec(memory_space=pltpu.VMEM)
    smem = pl.BlockSpec(memory_space=pltpu.SMEM)
    hbm = pl.BlockSpec(memory_space=pltpu.HBM)
    dma = pltpu.SemaphoreType.DMA
    block = (GROUP * 2 * S, TILE)
    echo, spec = pl.pallas_call(
        functools.partial(apply_kernel, nf, nt),
        out_shape=(
            jax.ShapeDtypeStruct((npos, 2 * S, TILE), F32),
            jax.ShapeDtypeStruct((freqs, 2 * S, cols), BF16),
        ),
        in_specs=[hbm, hbm, hbm, smem, smem, hbm],
        out_specs=(vmem, vmem),
        scratch_shapes=[
            pltpu.VMEM(recorded_seismograms.shape, BF16),
            pltpu.VMEM(left.shape, BF16),
            pltpu.VMEM(right.shape, BF16),
            pltpu.VMEM(ahead.shape[1:], BF16),
            pltpu.VMEM((freqs * 2 * S, count * S), BF16),
            pltpu.VMEM((2, nf // 2, 2 * S, cols), F32),
            pltpu.VMEM((2, nf // 2, 2 * S, cols), BF16),
            pltpu.VMEM((nf // 2, 2 * S, cols), BF16),
            pltpu.VMEM((nf // 2, 2 * S, cols), BF16),
            pltpu.VMEM((2 * S, cols), BF16),
            pltpu.VMEM((nt - 1, quads) + block, BF16),
            pltpu.VMEM((nt - 1, quads) + block, BF16),
            pltpu.VMEM((quads,) + block, F32),
            pltpu.VMEM((npos, 2 * S, TILE), F32),
            pltpu.VMEM((nt, quads) + block, BF16),
            pltpu.VMEM((2 * S, cols), F32),
            pltpu.VMEM((freqs, 2 * S, cols), BF16),
            dma((7,)),
            dma((2,)),
            dma((nf,)),
            dma((nf,)),
            dma((nt - 1, quads)),
            dma((nt - 1, quads)),
            dma((nt - 1, quads)),
            dma((nt - 1, quads)),
            dma((nf,)),
            dma((nf,)),
        ],
        compiler_params=pltpu.CompilerParams(
            collective_id=0, has_side_effects=True, vmem_limit_bytes=60 * 2**20
        ),
        name="apply",
    )(recorded_seismograms, left, right, rank_classes[0].T, owner, ahead)
    chunks = 4
    echo, synth = pl.pallas_call(
        functools.partial(synthesis_kernel, freqs),
        out_shape=(
            jax.ShapeDtypeStruct(echo.shape, F32),
            jax.ShapeDtypeStruct(recorded_seismograms.shape, BF16),
        ),
        in_specs=[vmem, vmem, hbm],
        out_specs=(hbm, hbm),
        scratch_shapes=[
            pltpu.VMEM(back.shape[1:], BF16),
            pltpu.VMEM((chunks, count // chunks, S, cols), BF16),
            dma((2 + chunks,)),
        ],
        compiler_params=pltpu.CompilerParams(vmem_limit_bytes=60 * 2**20),
        name="synthesis",
    )(spec, echo, back)
    return echo.reshape(1, npos, 2, S, TILE), synth


def solution(mesh):
    nf, nt = mesh.shape["freq"], mesh.shape["tile"]
    in_specs = (
        P("freq", None, "tile"),
        P("freq", None, "tile", None, None, None),
        P("freq", None, "tile", None, None, None),
        P("freq", None, "tile"),
        P(),
    )
    out_specs = (P("freq", "tile", None, None, None), P("freq", None, "tile"))
    return jax.shard_map(
        functools.partial(shards, nf, nt),
        mesh=mesh,
        in_specs=in_specs,
        out_specs=out_specs,
        check_vma=False,
    )
```

```python
import functools
import math

import jax
import jax.numpy as jnp
import numpy as np
from jax import lax
from jax.experimental import pallas as pl
from jax.experimental.pallas import tpu as pltpu
from jax.sharding import PartitionSpec as P

TILE = 256
RMAX = 32
S = 16
RECORD_LENGTH = 2048
LOW_BIN = 8
GROUP = 4
F32 = jnp.float32
BF16 = jnp.bfloat16
MESH = pl.DeviceIdType.MESH


def trig_tables(shards, count, freqs):
    bins = LOW_BIN + np.arange(freqs)
    angles = (bins[:, None] * np.arange(shards * count)[None, :] % RECORD_LENGTH) * (
        2.0 * math.pi / RECORD_LENGTH
    )
    both = np.stack([np.cos(angles), -np.sin(angles)], 1)
    both = both.reshape(2 * freqs, shards, count)
    near = both.reshape(freqs // 2, 2, 2, shards, count).swapaxes(0, 1)
    near = near.reshape(2 * freqs, shards, count)
    ahead = np.repeat(near.transpose(1, 0, 2), S, axis=2)
    back = np.repeat(both.transpose(1, 2, 0), S, axis=2)
    return jnp.asarray(ahead, BF16), jnp.asarray(back, BF16)


def partner(me, off, size):
    out = me
    bit = 1
    while bit < size:
        if off & bit:
            out = out + (1 - 2 * ((me // bit) % 2)) * bit
        bit *= 2
    return out


def nt_dot(a, b):
    return lax.dot_general(a, b, (((1,), (1,)), ((), ())), preferred_element_type=F32)


def nn_dot(a, b):
    return jnp.dot(a, b, preferred_element_type=F32)


def apply_kernel(
    nf,
    nt,
    x_hbm,
    l_hbm,
    r_hbm,
    rank_ref,
    owner_ref,
    ahead_hbm,
    echo_ref,
    spec_out,
    x_ref,
    l_ref,
    r_ref,
    ahead_ref,
    a_ref,
    acc_ref,
    part_ref,
    pair_ref,
    rs_ref,
    s_ref,
    send_ref,
    recv_ref,
    own_ref,
    rows_ref,
    adj_ref,
    gath_ref,
    load_sem,
    pair_sem,
    rs_send,
    rs_recv,
    row_send,
    row_recv,
    ag_send,
    ag_recv,
    sp_send,
    sp_recv,
):
    me_f = lax.axis_index("freq")
    me_t = lax.axis_index("tile")
    nz = nf // 2
    me_z, core = me_f // 2, me_f % 2
    sibling = me_f + 1 - 2 * core
    count = x_ref.shape[0]
    cols = x_ref.shape[2]
    col_tiles = l_ref.shape[1]
    freqs = nf
    npos = own_ref.shape[0]
    quads = npos // GROUP
    chunks = 4
    step_t = count // chunks
    kk = step_t * S

    ahead_copy = pltpu.make_async_copy(ahead_hbm.at[me_f], ahead_ref, load_sem.at[0])
    ahead_copy.start()
    x_copies = []
    for n in range(chunks):
        cp = pltpu.make_async_copy(
            x_hbm.at[pl.ds(n * step_t, step_t)], x_ref.at[pl.ds(n * step_t, step_t)], load_sem.at[1 + n]
        )
        cp.start()
        x_copies.append(cp)
    r_copy = pltpu.make_async_copy(r_hbm, r_ref, load_sem.at[1 + chunks])
    l_copy = pltpu.make_async_copy(l_hbm, l_ref, load_sem.at[2 + chunks])

    barrier = pltpu.get_barrier_semaphore()
    pl.semaphore_signal(barrier, inc=1, device_id=(sibling, me_t), device_id_type=MESH)
    for off in range(1, nz):
        pl.semaphore_signal(
            barrier,
            inc=1,
            device_id=(2 * partner(me_z, off, nz) + core, me_t),
            device_id_type=MESH,
        )
    two_level = nt == 4 and quads % 2 == 0
    offsets = (1, 2) if two_level else range(1, nt)
    barrier_count = nz + len(offsets)
    for off in offsets:
        pl.semaphore_signal(
            barrier, inc=1, device_id=(me_f, partner(me_t, off, nt)), device_id_type=MESH
        )

    ahead_copy.wait()
    diag = lax.broadcasted_iota(jnp.int32, (S, kk), 1) % S == lax.broadcasted_iota(
        jnp.int32, (S, kk), 0
    )
    total = 0.0
    for n in range(chunks):
        table = ahead_ref[:, n * kk : (n + 1) * kk].astype(F32)
        for k in range(2 * freqs):
            row = jnp.broadcast_to(table[k : k + 1], (S, kk))
            a_ref[k * S : (k + 1) * S, n * kk : (n + 1) * kk] = jnp.where(diag, row, 0.0).astype(
                BF16
            )
        x_copies[n].wait()
        if n == chunks - 2:
            r_copy.start()
            l_copy.start()
        block_x = x_ref[n * step_t : (n + 1) * step_t].reshape(kk, cols)
        total = total + nn_dot(a_ref[:, n * kk : (n + 1) * kk], block_x)
    total = (total * RECORD_LENGTH**-0.5).reshape(2, nz, 2 * S, cols)
    acc_ref[...] = total
    part_ref[...] = total.astype(BF16)

    pl.semaphore_wait(barrier, barrier_count)
    pair_copy = pltpu.make_async_remote_copy(
        src_ref=part_ref.at[1 - core],
        dst_ref=pair_ref,
        send_sem=pair_sem.at[0],
        recv_sem=pair_sem.at[1],
        device_id=(sibling, me_t),
        device_id_type=MESH,
    )
    pair_copy.start()
    adj_ref[...] = jnp.zeros_like(adj_ref)
    pair_copy.wait()
    summed = acc_ref[core] + pair_ref[...].astype(F32)
    acc_ref[core] = summed
    part_ref[core] = summed.astype(BF16)
    rs_copies = []
    for off in range(nz - 1, 0, -1):
        to = partner(me_z, off, nz)
        cp = pltpu.make_async_remote_copy(
            src_ref=part_ref.at[core, to],
            dst_ref=rs_ref.at[off],
            send_sem=rs_send.at[off],
            recv_sem=rs_recv.at[off],
            device_id=(2 * to + core, me_t),
            device_id_type=MESH,
        )
        cp.start()
        rs_copies.append((off, cp))
    spectra = acc_ref[core, me_z]
    for off, cp in reversed(rs_copies):
        cp.wait()
        spectra = spectra + rs_ref[off].astype(F32)
    s_ref[...] = spectra.astype(BF16)
    r_copy.wait()
    l_copy.wait()

    width = GROUP * RMAX
    lane = lax.broadcasted_iota(jnp.int32, (1, width), 1)
    lane_m = lane // RMAX
    lane_r = lane % RMAX
    block = (
        lax.broadcasted_iota(jnp.int32, (GROUP * 2 * S, width), 0) // (2 * S)
        == lax.broadcasted_iota(jnp.int32, (GROUP * 2 * S, width), 1) // RMAX
    )

    def gather(ref, idx, j, c):
        return [ref[i, j, c] for i in idx]

    def kept(idx, j):
        limit = jnp.zeros((1, width), jnp.int32)
        for m, i in enumerate(idx):
            value = (rank_ref[j, i] + 1) * (RMAX // 4)
            limit = jnp.where(lane_m == m, value, limit)
        return jnp.where(lane_r < limit, 1.0, 0.0).astype(F32)

    def forward(base):
        idx = [owner_ref[base + m] for m in range(GROUP)]
        left, weights = [], []
        for j in range(col_tiles):
            right = jnp.concatenate(gather(r_ref, idx, j, 0) + gather(r_ref, idx, j, 1), 0)
            p = nt_dot(s_ref[:, j * TILE : (j + 1) * TILE], right)
            keep = kept(idx, j)
            wr = (p[:S, :width] - p[S:, width:]) * keep
            wi = (p[S:, :width] + p[:S, width:]) * keep
            for first in ([wr, wi], [-wi, wr]):
                tiled = jnp.concatenate(first * GROUP, 0)
                weights.append(jnp.where(block, tiled, 0.0).astype(BF16))
            left += gather(l_ref, idx, j, 0) + gather(l_ref, idx, j, 1)
        return nn_dot(jnp.concatenate(weights, 1), jnp.concatenate(left, 0))

    def backward(base, rows):
        idx = [owner_ref[base + m] for m in range(GROUP)]
        left = []
        for j in range(col_tiles):
            left += gather(l_ref, idx, j, 0) + gather(l_ref, idx, j, 1)
        p = nt_dot(rows, jnp.concatenate(left, 0))
        for j in range(col_tiles):
            sums = []
            for c in range(2):
                at = (2 * j + c) * width
                q = jnp.where(block, p[:, at : at + width], 0.0)
                g = q[: 2 * S]
                for m in range(1, GROUP):
                    g = g + q[2 * S * m : 2 * S * (m + 1)]
                sums.append(g)
            keep = kept(idx, j)
            ar = (sums[0][:S] + sums[1][S:]) * keep
            ai = (sums[0][S:] - sums[1][:S]) * keep
            lhs = jnp.concatenate(
                [jnp.concatenate([ar, ai], 0), jnp.concatenate([ai, -ar], 0)], 1
            ).astype(BF16)
            right = jnp.concatenate(gather(r_ref, idx, j, 0) + gather(r_ref, idx, j, 1), 0)
            adj_ref[:, j * TILE : (j + 1) * TILE] += nn_dot(lhs, right)

    def row_copy(off, q):
        return pltpu.make_async_remote_copy(
            src_ref=send_ref.at[off - 1, q],
            dst_ref=recv_ref.at[off - 1, q],
            send_sem=row_send.at[off - 1, q],
            recv_sem=row_recv.at[off - 1, q],
            device_id=(me_f, partner(me_t, off, nt)),
            device_id_type=MESH,
        )

    def rows_copy(off, q):
        return pltpu.make_async_remote_copy(
            src_ref=rows_ref.at[0, q],
            dst_ref=rows_ref.at[off, q],
            send_sem=ag_send.at[off - 1, q],
            recv_sem=ag_recv.at[off - 1, q],
            device_id=(me_f, partner(me_t, off, nt)),
            device_id_type=MESH,
        )

    if two_level:

        def hop(src, dst, sems, k, q, off):
            return pltpu.make_async_remote_copy(
                src_ref=src,
                dst_ref=dst,
                send_sem=sems[0].at[k, q],
                recv_sem=sems[1].at[k, q],
                device_id=(me_f, partner(me_t, off, nt)),
                device_id_type=MESH,
            )

        def row_hop(k, q, off):
            return hop(send_ref.at[k, q], recv_ref.at[k, q], (row_send, row_recv), k, q, off)

        def ag_hop(k, q, src, off):
            return hop(rows_ref.at[src, q], rows_ref.at[k, q], (ag_send, ag_recv), k - 1, q, off)

        def base_of(off, q):
            return partner(me_t, off, nt) * npos + q * GROUP

        @pl.loop(0, quads // 2)
        def _(half):
            for first in (1, 2):
                q = 2 * half + first - 1
                send_ref[0, q] = forward(base_of(3, q)).astype(BF16)
                row_hop(0, q, first).start()

        @pl.loop(0, quads // 2)
        def _(half):
            for first in (1, 2):
                q = 2 * half + first - 1
                send_ref[1, q] = forward(base_of(first, q)).astype(BF16)
                row_hop(1, q, first).start()
            for first in (1, 2):
                q = 2 * half + first - 1
                mid = forward(base_of(3 - first, q))
                row_hop(0, q, first).wait()
                send_ref[2, q] = (mid + recv_ref[0, q].astype(F32)).astype(BF16)
                row_hop(2, q, 3 - first).start()

        @pl.loop(0, quads // 2)
        def _(half):
            for first in (1, 2):
                q = 2 * half + first - 1
                out = forward(base_of(0, q))
                own_ref[pl.ds(q * GROUP, GROUP)] = out.reshape(GROUP, 2 * S, TILE)

        @pl.loop(0, quads // 2)
        def _(half):
            for first in (1, 2):
                q = 2 * half + first - 1
                rows = own_ref[pl.ds(q * GROUP, GROUP)].reshape(GROUP * 2 * S, TILE)
                row_hop(1, q, first).wait()
                row_hop(2, q, 3 - first).wait()
                rows = rows + recv_ref[1, q].astype(F32) + recv_ref[2, q].astype(F32)
                echo_ref[pl.ds(q * GROUP, GROUP)] = rows.reshape(GROUP, 2 * S, TILE)
                low = rows.astype(BF16)
                rows_ref[0, q] = low
                ag_hop(first, q, 0, first).start()
                ag_hop(3 - first, q, 0, 3 - first).start()
                backward(base_of(0, q), low)

        @pl.loop(0, quads // 2)
        def _(half):
            for first in (1, 2):
                q = 2 * half + first - 1
                ag_hop(first, q, 0, first).wait()
                ag_hop(3, q, first, 3 - first).start()
                ag_hop(3 - first, q, 0, 3 - first).wait()
                backward(base_of(first, q), rows_ref[first, q])
                backward(base_of(3 - first, q), rows_ref[3 - first, q])

        @pl.loop(0, quads // 2)
        def _(half):
            for first in (1, 2):
                q = 2 * half + first - 1
                ag_hop(3, q, first, 3 - first).wait()
                backward(base_of(3, q), rows_ref[3, q])

    else:

        @pl.loop(0, quads)
        def _(q):
            for off in range(nt - 1, 0, -1):
                out = forward(partner(me_t, off, nt) * npos + q * GROUP)
                send_ref[off - 1, q] = out.astype(BF16)
                row_copy(off, q).start()
            out = forward(me_t * npos + q * GROUP)
            own_ref[pl.ds(q * GROUP, GROUP)] = out.reshape(GROUP, 2 * S, TILE)

        @pl.loop(0, quads)
        def _(q):
            rows = own_ref[pl.ds(q * GROUP, GROUP)].reshape(GROUP * 2 * S, TILE)
            for off in range(1, nt):
                row_copy(off, q).wait()
                rows = rows + recv_ref[off - 1, q].astype(F32)
            echo_ref[pl.ds(q * GROUP, GROUP)] = rows.reshape(GROUP, 2 * S, TILE)
            low = rows.astype(BF16)
            rows_ref[0, q] = low
            for off in range(nt - 1, 0, -1):
                rows_copy(off, q).start()
            backward(me_t * npos + q * GROUP, low)

        @pl.loop(0, quads)
        def _(q):
            for off in range(1, nt):
                rows_copy(off, q).wait()
                backward(partner(me_t, off, nt) * npos + q * GROUP, rows_ref[off, q])

    gath_ref[me_f] = adj_ref[...].astype(BF16)

    def spec_copy(n, at, to):
        return pltpu.make_async_remote_copy(
            src_ref=gath_ref.at[at],
            dst_ref=gath_ref.at[at],
            send_sem=sp_send.at[n],
            recv_sem=sp_recv.at[n],
            device_id=(to, me_t),
            device_id_type=MESH,
        )

    sp_copies = []
    for off in range(nz - 1, 0, -1):
        to = 2 * partner(me_z, off, nz) + core
        cp = spec_copy(off, me_f, to)
        cp.start()
        sp_copies.append((off, to, cp))
    last = [spec_copy(nz, me_f, sibling)]
    last[0].start()
    for off, to, cp in reversed(sp_copies):
        cp.wait()
        last.append(spec_copy(nz + off, to, sibling))
        last[-1].start()
    for cp in last:
        cp.wait()
    spec_out[...] = gath_ref[...]


def synthesis_kernel(
    freqs, spec_hbm, echo_in, back_hbm, echo_out, out_hbm, spec_ref, echo_ref, back_ref, out_ref, sem
):
    me_f = lax.axis_index("freq")
    count, cols = out_hbm.shape[0], out_hbm.shape[2]
    chunks = out_ref.shape[0]
    step_t = count // chunks
    lanes = back_ref.shape[1]
    back_copy = pltpu.make_async_copy(back_hbm.at[me_f], back_ref, sem.at[0])
    back_copy.start()
    spec_copy = pltpu.make_async_copy(spec_hbm, spec_ref, sem.at[1])
    spec_copy.start()
    echo_load = pltpu.make_async_copy(echo_in, echo_ref, sem.at[2])
    echo_load.start()
    diag = lax.broadcasted_iota(jnp.int32, (S, lanes), 1) % S == lax.broadcasted_iota(
        jnp.int32, (S, lanes), 0
    )
    back_copy.wait()
    spec_copy.wait()
    spec = spec_ref[...].reshape(lanes, cols)
    copies = []
    for n in range(chunks):
        table = back_ref[n * step_t : (n + 1) * step_t].astype(F32)
        spread = jnp.where(diag[None], table[:, None, :], 0.0).astype(BF16)
        out = nn_dot(spread.reshape(step_t * S, lanes), spec) * freqs**-0.5
        out_ref[n] = out.reshape(step_t, S, cols).astype(BF16)
        cp = pltpu.make_async_copy(
            out_ref.at[n], out_hbm.at[pl.ds(n * step_t, step_t)], sem.at[4 + n]
        )
        cp.start()
        copies.append(cp)
    echo_load.wait()
    echo_copy = pltpu.make_async_copy(echo_ref, echo_out, sem.at[3])
    echo_copy.start()
    for cp in copies:
        cp.wait()
    echo_copy.wait()


def shards(nf, nt, recorded_seismograms, left_bases, right_bases, rank_classes, owner):
    count, _, cols = recorded_seismograms.shape
    per_device, row_tiles, col_tiles = left_bases.shape[:3]
    assert per_device == 1
    freqs = per_device * nf
    npos = row_tiles // nt
    quads = npos // GROUP
    left = left_bases.reshape(left_bases.shape[1:])
    right = right_bases.reshape(right_bases.shape[1:])
    ahead, back = trig_tables(nf, count, freqs)
    vmem = pl.BlockSpec(memory_space=pltpu.VMEM)
    smem = pl.BlockSpec(memory_space=pltpu.SMEM)
    hbm = pl.BlockSpec(memory_space=pltpu.HBM)
    dma = pltpu.SemaphoreType.DMA
    block = (GROUP * 2 * S, TILE)
    echo, spec = pl.pallas_call(
        functools.partial(apply_kernel, nf, nt),
        out_shape=(
            jax.ShapeDtypeStruct((npos, 2 * S, TILE), F32),
            jax.ShapeDtypeStruct((freqs, 2 * S, cols), BF16),
        ),
        in_specs=[hbm, hbm, hbm, smem, smem, hbm],
        out_specs=(vmem, vmem),
        scratch_shapes=[
            pltpu.VMEM(recorded_seismograms.shape, BF16),
            pltpu.VMEM(left.shape, BF16),
            pltpu.VMEM(right.shape, BF16),
            pltpu.VMEM(ahead.shape[1:], BF16),
            pltpu.VMEM((freqs * 2 * S, count * S), BF16),
            pltpu.VMEM((2, nf // 2, 2 * S, cols), F32),
            pltpu.VMEM((2, nf // 2, 2 * S, cols), BF16),
            pltpu.VMEM((nf // 2, 2 * S, cols), BF16),
            pltpu.VMEM((nf // 2, 2 * S, cols), BF16),
            pltpu.VMEM((2 * S, cols), BF16),
            pltpu.VMEM((nt - 1, quads) + block, BF16),
            pltpu.VMEM((nt - 1, quads) + block, BF16),
            pltpu.VMEM((npos, 2 * S, TILE), F32),
            pltpu.VMEM((nt, quads) + block, BF16),
            pltpu.VMEM((2 * S, cols), F32),
            pltpu.VMEM((freqs, 2 * S, cols), BF16),
            dma((7,)),
            dma((2,)),
            dma((nf,)),
            dma((nf,)),
            dma((nt - 1, quads)),
            dma((nt - 1, quads)),
            dma((nt - 1, quads)),
            dma((nt - 1, quads)),
            dma((nf,)),
            dma((nf,)),
        ],
        compiler_params=pltpu.CompilerParams(
            collective_id=0, has_side_effects=True, vmem_limit_bytes=60 * 2**20
        ),
        name="apply",
    )(recorded_seismograms, left, right, rank_classes[0].T, owner, ahead)
    chunks = 8
    echo, synth = pl.pallas_call(
        functools.partial(synthesis_kernel, freqs),
        out_shape=(
            jax.ShapeDtypeStruct(echo.shape, F32),
            jax.ShapeDtypeStruct(recorded_seismograms.shape, BF16),
        ),
        in_specs=[hbm, hbm, hbm],
        out_specs=(hbm, hbm),
        scratch_shapes=[
            pltpu.VMEM(spec.shape, BF16),
            pltpu.VMEM(echo.shape, F32),
            pltpu.VMEM(back.shape[1:], BF16),
            pltpu.VMEM((chunks, count // chunks, S, cols), BF16),
            dma((4 + chunks,)),
        ],
        compiler_params=pltpu.CompilerParams(vmem_limit_bytes=60 * 2**20),
        name="synthesis",
    )(spec, echo, back)
    return echo.reshape(1, npos, 2, S, TILE), synth


def solution(mesh):
    nf, nt = mesh.shape["freq"], mesh.shape["tile"]
    in_specs = (
        P("freq", None, "tile"),
        P("freq", None, "tile", None, None, None),
        P("freq", None, "tile", None, None, None),
        P("freq", None, "tile"),
        P(),
    )
    out_specs = (P("freq", "tile", None, None, None), P("freq", None, "tile"))
    return jax.shard_map(
        functools.partial(shards, nf, nt),
        mesh=mesh,
        in_specs=in_specs,
        out_specs=out_specs,
        check_vma=False,
    )
```
